32 devices in a mesh: seq: 8 (over z, y), head: 4 (over x, core).
Axes of the slice: x: 2, y: 2, z: 4, core: 2. Of those that a mesh axis runs over, the one named last changes fastest.
Arguments:
- queries: bfloat16 [8192, 4096], P('seq', 'head'), may hold values from -6 to 6
- keys: bfloat16 [8192, 4096], P('seq', 'head'), may hold values from -6 to 6
- values: bfloat16 [8192, 4096], P('seq', 'head'), may hold values from -6 to 6
- decay: float32 [8192, 4096], P('seq', 'head'), as said below
- beta: float32 [32, 8192], P('head', 'seq'), may hold values from 0.002 to 0.98
- wy_inverse: float32 [128, 64, 2048], P('seq', None, 'head')
- out_gate: bfloat16 [8192, 4096], P('seq', 'head'), may hold values from -6 to 6
- norm_gain: float32 [128], replicated, may hold values from 0.1 to 1.9
- out_proj: bfloat16 [4096, 2304], P('head'), may hold values from -0.125 to 0.125
- grad_out: bfloat16 [8192, 2304], P('seq', 'head'), may hold values from -6 to 6
- resets: int32 [8], P('seq'), may hold values from 0 to 16, as said below
Outputs:
- grad_queries: bfloat16 [8192, 4096], P('seq', 'head')
- grad_keys: bfloat16 [8192, 4096], P('seq', 'head')
- grad_values: bfloat16 [8192, 4096], P('seq', 'head')
- grad_decay: float32 [8192, 4096], P('seq', 'head')
- grad_beta: float32 [32, 8192], P('head', 'seq')
- grad_gate: bfloat16 [8192, 4096], P('seq', 'head')
The draws below stay inside these ranges and needn't reach their ends.
Inputs may be any that keep to these rules, and one draw needn't show every extreme that they name: `resets`: 16 means that no document starts in that index of seq; the first value is 0 and the last is 16. Natural logarithms of decay factors, at most 0.
All inputs are finite; a program needn't handle non-finite values.
Results may differ from the reference program's by a relative error of at most 0.02.
Values may be sent and summed in bfloat16 or wider, within the bound.
A program may use at most 192 MiB of HBM per device.

```python
import math
import jax
import jax.numpy as jnp
from jax import lax

H = 32
DK = 128
DV = 128
D = 2304
GROUP = 64
TOK_DEV = 1024
TOKENS = 8192
CH_DEV = 16


def shared_fields(key, slow_share):
    key_keys = jax.random.fold_in(key, 101)
    key_decay = jax.random.fold_in(key, 102)
    key_beta = jax.random.fold_in(key, 103)
    columns = H * DK
    keys_f = jnp.clip(jax.random.normal(key_keys, (TOKENS, columns)), -6.0, 6.0)
    keys_f = keys_f.astype(jnp.bfloat16).astype(jnp.float32)
    parts = jax.random.split(key_decay, 7)
    slow = jax.random.uniform(parts[0], (columns,)) < slow_share
    slow_rate = jnp.exp(jax.random.uniform(parts[1], (columns,), minval=math.log(0.02 / TOKENS), maxval=math.log(0.2 / TOKENS)))
    fast_rate = jax.random.uniform(parts[2], (columns,), minval=1.0 / 50.0, maxval=1.0 / 30.0)
    baseline_level = jnp.where(slow, slow_rate, fast_rate)
    coarse_estimate = jax.random.uniform(parts[3], (TOKENS, columns), minval=0.5, maxval=1.5)
    blocks_count = TOKENS // TOK_DEV
    multiplier_term = jnp.exp(jax.random.uniform(parts[4], (blocks_count,), minval=math.log(0.5), maxval=math.log(2.0)))
    multiplier_term = jnp.repeat(multiplier_term, TOK_DEV)[:, None]
    reset_locations = jax.random.randint(parts[5], (2,), 0, TOKENS)
    loss_values = jnp.log(jax.random.uniform(parts[6], (2,), minval=0.6, maxval=0.8))
    token_positions = jnp.arange(TOKENS)[:, None]
    spike_amount = jnp.sum(jnp.where(token_positions == reset_locations[None, :], loss_values[None, :], 0.0), axis=1)[:, None]
    decay = (-baseline_level[None, :] * coarse_estimate * multiplier_term + spike_amount).astype(jnp.float32)
    beta_keys = jax.random.split(key_beta, 3)
    quiet = jax.random.uniform(beta_keys[0], (H,)) < 0.5
    center = jnp.where(quiet, -5.5, jax.random.uniform(beta_keys[1], (H,), minval=-1.0, maxval=1.5))
    spread = jnp.where(quiet, 1.0, 1.5)
    noise = jax.random.normal(beta_keys[2], (H, TOKENS))
    beta = jnp.clip(jax.nn.sigmoid(center[:, None] + spread[:, None] * noise), 0.002, 0.98)
    return (keys_f, decay, beta.astype(jnp.float32))


def block_inverse(keys_f, decay, beta):
    count = TOKENS // GROUP
    rows = keys_f.reshape(TOKENS, H, DK)
    unit = rows * lax.rsqrt(jnp.sum(rows * rows, axis=-1, keepdims=True) + 1e-06)
    unit = unit.reshape(count, GROUP, H, DK).transpose(0, 2, 1, 3)
    gates = decay.reshape(count, GROUP, H, DK).transpose(0, 2, 1, 3)
    cumul = jnp.cumsum(gates, axis=2)
    key_dec = unit * jnp.exp(cumul)
    key_inv = unit * jnp.exp(-cumul)
    strength = beta.reshape(H, count, GROUP).transpose(1, 0, 2)
    strict = jnp.einsum('chid,chjd->chij', key_dec, key_inv, precision=lax.Precision.HIGHEST)
    strict = strict * strength[:, :, :, None]
    below = (jnp.arange(GROUP)[None, :] < jnp.arange(GROUP)[:, None]).astype(jnp.float32)
    strict = strict * below
    eye = jnp.eye(GROUP, dtype=jnp.float32)
    start = jnp.broadcast_to(eye, strict.shape)

    def solve_row(index, result):
        coeffs = lax.dynamic_index_in_dim(strict, index, 2, keepdims=False)
        row = lax.dynamic_index_in_dim(eye, index, 0, keepdims=False)
        row = row - jnp.einsum('chj,chjk->chk', coeffs, result, precision=lax.Precision.HIGHEST)
        return lax.dynamic_update_index_in_dim(result, row, index, 2)
    inverse = lax.fori_loop(0, GROUP, solve_row, start)
    return inverse.transpose(0, 2, 1, 3).reshape(count, GROUP, H * GROUP).astype(jnp.float32)


def draw_keys(key, part):
    fields = shared_fields(key, 0.5)
    return fields[0].astype(jnp.bfloat16)


def draw_beta(key, part):
    fields = shared_fields(key, 0.5)
    return fields[2].astype(jnp.float32)


def draw_decay(key, part):
    fields = shared_fields(key, 0.5)
    return fields[1].astype(jnp.float32)


def draw_wy_inverse(key, part):
    fields = shared_fields(key, 0.5)
    return block_inverse(fields[0], fields[1], fields[2])


def draw_resets(key, part):
    key = jax.random.fold_in(key, 11)
    blocks_count = TOKENS // TOK_DEV
    drawn_starts = jax.random.randint(key, (blocks_count,), 0, 4 * CH_DEV)
    chosen = jnp.where(drawn_starts < CH_DEV, drawn_starts, CH_DEV)
    reset_locations = jnp.arange(blocks_count)
    chosen = jnp.where(reset_locations == 0, 0, jnp.where(reset_locations == blocks_count - 1, CH_DEV, chosen))
    return chosen.astype(jnp.int32)


def levels(rng, extent, shards, smallest, largest):
    factor_of = 1.0
    for position, blocks in shards:
        heights = jax.random.uniform(jax.random.fold_in(jax.random.fold_in(rng, 6), position), (blocks,), jnp.float32, smallest / len(shards), largest / len(shards))
        factor_of = factor_of * jnp.repeat(jnp.exp(heights), extent[position] // blocks).reshape((-1,) + (1,) * (len(extent) - 1 - position))
    return factor_of


def scatter_about(own_key, dims, scale, bound, shards=(), kind=jnp.bfloat16):
    level = levels(own_key, dims, shards, -0.22, 0.18) if shards else 1.0
    values = jax.random.normal(own_key, dims, jnp.float32) * scale * level
    return jnp.minimum(jnp.maximum(values, -bound), bound).astype(kind)


def setup_inputs(seed: int = 0) -> dict:
    arg_keys = jax.random.split(jax.random.key(seed), 12)
    return {
        "queries": scatter_about(arg_keys[0], (TOKENS, H * DK), 1.0, 6.0, ((0, 8), (1, 4))),
        "keys": draw_keys(jax.random.fold_in(arg_keys[11], 71), 0),
        "values": scatter_about(arg_keys[2], (TOKENS, H * DV), 1.0, 6.0, ((0, 8), (1, 4))),
        "decay": draw_decay(jax.random.fold_in(arg_keys[11], 71), 0),
        "beta": draw_beta(jax.random.fold_in(arg_keys[11], 71), 0),
        "wy_inverse": draw_wy_inverse(jax.random.fold_in(arg_keys[11], 71), 0),
        "out_gate": scatter_about(arg_keys[6], (TOKENS, H * DV), 1.0, 6.0, ((0, 8), (1, 4))),
        "norm_gain": jnp.clip(1.0 + 0.18 * jax.random.normal(arg_keys[7], (DV,), jnp.float32), 0.1, 1.9),
        "out_proj": scatter_about(arg_keys[8], (H * DV, D), D ** -0.5, 0.125, ((0, 4),)),
        "grad_out": scatter_about(arg_keys[9], (TOKENS, D), 1.0, 6.0, ((0, 8), (1, 4))),
        "resets": draw_resets(jax.random.fold_in(arg_keys[11], 71), 0),
    }


precise = lax.Precision.HIGHEST

def to_blocks(array, heads, width):
    count = array.shape[0] // GROUP
    return array.reshape(count, GROUP, heads, width).transpose(0, 2, 1, 3)

def from_blocks(array):
    count, heads, length, width = array.shape
    return array.transpose(0, 2, 1, 3).reshape(count * length, heads * width)

def unit_rows(array, width, multiplier_term):
    rows = array.reshape(array.shape[0], -1, width)
    scale = lax.rsqrt(lax.optimization_barrier(jnp.sum(rows * rows, axis=-1, keepdims=True)) + 1e-06)
    return (rows * scale * multiplier_term).reshape(array.shape)

def low_product(form, left, right):
    return jnp.einsum(form, left.astype(jnp.bfloat16), right.astype(jnp.bfloat16), preferred_element_type=jnp.float32)

def group_step(state, block):
    query_rows, key_rows, value_rows, gate_rows, beta_rows, wy_rows, keep_flag = block
    entry = state * keep_flag
    cumul = jnp.cumsum(gate_rows, axis=1)
    final = cumul[:, -1:, :]
    query_dec = query_rows * jnp.exp(cumul)
    key_dec = key_rows * jnp.exp(cumul)
    key_inv = key_rows * jnp.exp(-cumul)
    key_tail = key_rows * jnp.exp(final - cumul)
    lower = jnp.tril(jnp.ones((GROUP, GROUP), jnp.float32))
    predicted = jnp.einsum('hld,hdv->hlv', key_dec, entry, precision=precise)
    target = beta_rows[:, :, None] * (value_rows - predicted)
    update = low_product('hij,hjv->hiv', wy_rows, target)
    scores = low_product('hid,hjd->hij', query_dec, key_inv) * lower
    output = jnp.einsum('hld,hdv->hlv', query_dec, entry, precision=precise)
    output = output + low_product('hij,hjv->hiv', scores, update)
    carried = jnp.exp(final[:, 0, :])[:, :, None] * entry
    carried = carried + low_product('hld,hlv->hdv', key_tail, update)
    return (carried, output)

def core(query_unit, key_unit, value_f, decay, beta, wy_inverse, keep, state, stepper):
    heads = beta.shape[0]
    count = query_unit.shape[0] // GROUP
    blocks = (to_blocks(query_unit, heads, DK), to_blocks(key_unit, heads, DK), to_blocks(value_f, heads, DV), to_blocks(decay, heads, DK), beta.reshape(heads, count, GROUP).transpose(1, 0, 2), wy_inverse.reshape(count, GROUP, heads, GROUP).transpose(0, 2, 1, 3), keep)
    final, outputs = lax.scan(stepper, state, blocks)
    return (from_blocks(outputs), final)

def gated_norm(output, gate, gain):
    rows = output.reshape(output.shape[0], -1, DV)
    scale = lax.rsqrt(lax.optimization_barrier(jnp.mean(rows * rows, axis=-1, keepdims=True)) + 1e-06)
    gates = jax.nn.sigmoid(gate.reshape(rows.shape))
    return (rows * scale * gain * gates).reshape(output.shape)

def reference(queries, keys, values, decay, beta, wy_inverse, out_gate, norm_gain, out_proj, grad_out, resets):
    upstream = jnp.dot(grad_out, out_proj.T, preferred_element_type=jnp.float32)
    count = queries.shape[0] // GROUP
    blocks_idx = jnp.arange(count)
    starts = resets[(blocks_idx // CH_DEV).astype(jnp.int32)]
    keep = ((blocks_idx % CH_DEV).astype(jnp.int32) != starts).astype(jnp.float32)
    anchor = jnp.zeros((H, DK, DV), jnp.float32)
    stepper = jax.checkpoint(group_step)

    def layer(query_f, key_f, value_f, gate_log, beta_f, gate_f):
        query_unit = unit_rows(query_f, DK, DK ** (-0.5))
        key_unit = unit_rows(key_f, DK, 1.0)
        output, final = core(query_unit, key_unit, value_f, gate_log, beta_f, wy_inverse, keep, anchor, stepper)
        return gated_norm(output, gate_f, norm_gain)
    normed, pullback = jax.vjp(layer, queries.astype(jnp.float32), keys.astype(jnp.float32), values.astype(jnp.float32), decay, beta, out_gate.astype(jnp.float32))
    grads = pullback(upstream)
    return (grads[0].astype(jnp.bfloat16), grads[1].astype(jnp.bfloat16), grads[2].astype(jnp.bfloat16), grads[3], grads[4], grads[5].astype(jnp.bfloat16))
```

```python
import functools

import jax
import jax.numpy as jnp
from jax import lax
from jax.experimental import pallas as pl
from jax.experimental.pallas import tpu as pltpu
from jax.sharding import PartitionSpec as P

DK = 128
DV = 128
GROUP = 64
SCALE = DK ** (-0.5)
MESH = pl.DeviceIdType.MESH
VMEM_LIMIT = 48 * 1024 * 1024
f32 = jnp.float32
bf16 = jnp.bfloat16


def nn(a, b):
    return lax.dot_general(
        a.astype(bf16), b.astype(bf16), (((1,), (0,)), ((), ())), preferred_element_type=f32
    )


def nt(a, b):
    return lax.dot_general(
        a.astype(bf16), b.astype(bf16), (((1,), (1,)), ((), ())), preferred_element_type=f32
    )


def tn(a, b):
    return lax.dot_general(
        a.astype(bf16), b.astype(bf16), (((0,), (0,)), ((), ())), preferred_element_type=f32
    )


def triangle(upper, copies):
    rows = lax.broadcasted_iota(jnp.int32, (GROUP, GROUP), 0)
    cols = lax.broadcasted_iota(jnp.int32, (GROUP, GROUP), 1)
    keep = (cols >= rows) if upper else (cols <= rows)
    one = keep.astype(f32).astype(bf16)
    return jnp.concatenate([one] * copies, axis=1)


def lower_only(x):
    rows = lax.broadcasted_iota(jnp.int32, x.shape, 0)
    cols = lax.broadcasted_iota(jnp.int32, x.shape, 1)
    return jnp.where(cols <= rows, x, 0.0)


def split_rows(x, parts):
    out = []
    for _ in range(parts):
        piece = x.astype(bf16)
        out.append(piece)
        x = x - piece.astype(f32)
    return jnp.concatenate(out, axis=0)


def cumulative(decay):
    return nn(triangle(False, 3), split_rows(decay, 3))


def unit(x):
    scale = lax.rsqrt(jnp.sum(x * x, axis=-1, keepdims=True) + 1e-06)
    return x * scale, scale


def local_kernel(
    heads, together, resets, q_ref, k_ref, v_ref, g_ref, b_ref, w_ref,
    out_ref, map_ref, enter_ref, total_ref, state,
):
    step = pl.program_id(0)

    @pl.when(step == 0)
    def _():
        eye = (
            lax.broadcasted_iota(jnp.int32, (DK, DK), 0)
            == lax.broadcasted_iota(jnp.int32, (DK, DK), 1)
        ).astype(f32)
        for h in range(heads):
            state[h, :DV] = jnp.zeros((DV, DK), f32)
            state[h, DV:] = eye

    keep = jnp.where(step == resets[0], 0.0, 1.0)
    cumul = cumulative(g_ref[...])
    grow = jnp.exp(cumul)
    shrink = jnp.exp(-cumul)
    for first in range(0, heads, together):
        hs = list(range(first, first + together))
        cols = {h: slice(h * DK, (h + 1) * DK) for h in hs}
        entry, both, inv, tail, low, pred, scores, target, update = ({} for _ in range(9))
        for h in hs:
            entry[h] = state[h] * keep
            enter_ref[0, h] = entry[h].astype(bf16)
            qu = unit(q_ref[:, cols[h]].astype(f32))[0] * SCALE
            ku = unit(k_ref[:, cols[h]].astype(f32))[0]
            up = grow[:, cols[h]]
            both[h] = jnp.concatenate([(ku * up).astype(bf16), (qu * up).astype(bf16)], axis=0)
            ki = ku * shrink[:, cols[h]]
            inv[h] = ki.astype(bf16)
            tail[h] = (ki * up[GROUP - 1 :]).astype(bf16)
        for h in hs:
            pred[h] = nt(both[h], entry[h])
            scores[h] = lower_only(nt(both[h][GROUP:], inv[h]))
        for h in hs:
            beta = b_ref[:, h : h + 1]
            value = v_ref[:, cols[h]].astype(f32)
            top = pred[h][:GROUP]
            target[h] = jnp.concatenate(
                [beta * (value - top[:, :DV]), -(beta * top[:, DV:])], axis=1
            )
        for h in hs:
            update[h] = nn(w_ref[0, :, h * GROUP : (h + 1) * GROUP], target[h]).astype(bf16)
        for h in hs:
            result = pred[h][GROUP:] + nn(scores[h], update[h])
            out_ref[:, cols[h]] = result[:, :DV]
            map_ref[:, cols[h]] = result[:, DV:].astype(bf16)
            up = grow[GROUP - 1 :, cols[h]]
            state[h] = entry[h] * up + tn(update[h], tail[h])

    @pl.when(step == pl.num_programs(0) - 1)
    def _():
        total_ref[...] = state[...]


def relay_kernel(n, forward, map_ref, add_ref, out_ref, arrive, depart, send_sem, recv_sem):
    me = lax.axis_index("seq")
    heads = out_ref.shape[0]
    if forward:
        has_source, has_target = me > 0, me < n - 1
        source, target = me - 1, me + 1
    else:
        has_source, has_target = me < n - 1, me > 0
        source, target = me + 1, me - 1

    barrier = pltpu.get_barrier_semaphore()

    @pl.when(has_source)
    def _():
        pl.semaphore_signal(barrier, inc=1, device_id={"seq": source}, device_id_type=MESH)

    @pl.when(has_target)
    def _():
        pl.semaphore_signal(barrier, inc=1, device_id={"seq": target}, device_id_type=MESH)

    @pl.when(jnp.logical_and(me > 0, me < n - 1))
    def _():
        pl.semaphore_wait(barrier, 2)

    if n > 1:
        @pl.when(jnp.logical_or(me == 0, me == n - 1))
        def _():
            pl.semaphore_wait(barrier, 1)

    def copy(h):
        return pltpu.make_async_remote_copy(
            src_ref=depart.at[h],
            dst_ref=arrive.at[h],
            send_sem=send_sem.at[h],
            recv_sem=recv_sem.at[h],
            device_id={"seq": target},
            device_id_type=MESH,
        )

    @pl.when(jnp.logical_not(has_source))
    def _():
        out_ref[...] = jnp.zeros_like(out_ref)

    for h in range(heads):
        @pl.when(has_source)
        def _():
            copy(h).wait_recv()
            out_ref[h] = arrive[h]

        @pl.when(has_target)
        def _():
            matrix = map_ref[h, DV:]
            high = matrix.astype(bf16)
            rest = matrix - high.astype(f32)
            now = out_ref[h]
            times = nn if forward else nt
            depart[h] = (add_ref[h, :DV] + (times(now, high) + times(now, rest))).astype(bf16)
            copy(h).start()

    @pl.when(has_target)
    def _():
        for h in range(heads):
            copy(h).wait_send()


def norm_kernel(in_ref, map_ref, s_ref, up_ref, gate_ref, gain_ref, go_ref, gg_ref, rest_ref):
    maps = map_ref[...]
    out = in_ref[...] + nt(maps, s_ref[0])
    scale = lax.rsqrt(jnp.mean(out * out, axis=-1, keepdims=True) + 1e-06)
    normal = out * scale
    sig = jax.nn.sigmoid(gate_ref[...].astype(f32))
    grad = up_ref[...] * gain_ref[...] * sig
    gg_ref[...] = (grad * normal * (1.0 - sig)).astype(bf16)
    inner = jnp.mean(grad * normal, axis=-1, keepdims=True)
    grad_out = (scale * (grad - normal * inner)).astype(bf16)
    go_ref[...] = grad_out
    rest_ref[0] = tn(grad_out, maps)


def grad_kernel(
    heads, together, resets, q_ref, k_ref, v_ref, g_ref, b_ref, w_ref, go_ref, enter_ref, s_ref,
    ds_ref, gq_ref, gk_ref, gv_ref, gd_ref, gb_ref, state,
):
    step = pl.program_id(0)
    chunk = pl.num_programs(0) - 1 - step

    @pl.when(step == 0)
    def _():
        state[...] = ds_ref[...].astype(f32)

    keep = jnp.where(chunk == resets[0], 0.0, 1.0)
    cumul = cumulative(g_ref[...])
    grow = jnp.exp(cumul)
    shrink = jnp.exp(-cumul)
    slopes = []
    for first in range(0, heads, together):
        hs = list(range(first, first + together))
        cols = {h: slice(h * DK, (h + 1) * DK) for h in hs}
        (entry, qd, kd, ki, kt, qh, kh, qs, ks, lows, err, update, scores, dscore, dup, dtar, dval,
         gout, past, dq, dk, di, dt, nxt, w) = ({} for _ in range(25))
        for h in hs:
            half = enter_ref[0, h]
            entry[h] = half[:DV].astype(f32) + nn(s_ref[h], half[DV:])
            qh[h], qs[h] = unit(q_ref[:, cols[h]].astype(f32))
            kh[h], ks[h] = unit(k_ref[:, cols[h]].astype(f32))
            up = grow[:, cols[h]]
            qd[h] = qh[h] * SCALE * up
            kd[h] = kh[h] * up
            ki[h] = kh[h] * shrink[:, cols[h]]
            kt[h] = ki[h] * up[GROUP - 1 :]
            gout[h] = go_ref[:, cols[h]]
            w[h] = w_ref[0, :, h * GROUP : (h + 1) * GROUP].astype(bf16)
            nxt[h] = state[h]
        for h in hs:
            lows[h] = entry[h].astype(bf16)
            scores[h] = lower_only(nt(qd[h], ki[h])).astype(bf16)
            err[h] = v_ref[:, cols[h]].astype(f32) - nt(kd[h], lows[h])
        for h in hs:
            update[h] = nn(w[h], b_ref[:, h : h + 1] * err[h]).astype(bf16)
            dup[h] = tn(scores[h], gout[h]) + nt(kt[h], nxt[h])
        for h in hs:
            dtar[h] = tn(w[h], dup[h])
            dscore[h] = lower_only(nt(gout[h], update[h])).astype(bf16)
        for h in hs:
            dval[h] = b_ref[:, h : h + 1] * dtar[h]
            gv_ref[:, cols[h]] = dval[h].astype(bf16)
            gb_ref[:, h : h + 1] = jnp.sum(dtar[h] * err[h], axis=-1, keepdims=True)
        for h in hs:
            both = jnp.concatenate([gout[h], -dval[h].astype(bf16)], axis=0)
            back = jnp.concatenate([qd[h].astype(bf16), kd[h].astype(bf16)], axis=0)
            up = grow[GROUP - 1 :, cols[h]]
            past[h] = nxt[h] * up
            state[h] = (past[h] + tn(both, back)) * keep
            through = nn(both, lows[h])
            dq[h] = through[:GROUP] + nn(dscore[h], ki[h])
            dk[h] = through[GROUP:]
            di[h] = tn(dscore[h], qd[h])
            dt[h] = nn(update[h], nxt[h])
        for h in hs:
            up = grow[:, cols[h]]
            tailed = dt[h] * kt[h]
            last = jnp.sum(past[h] * entry[h], axis=0, keepdims=True) + jnp.sum(
                tailed, axis=0, keepdims=True
            )
            slope = dq[h] * qd[h] + dk[h] * kd[h] - di[h] * ki[h] - tailed
            slopes.append((slope, last))
            gq = dq[h] * up
            gk = dk[h] * up + (di[h] + dt[h] * up[GROUP - 1 :]) * shrink[:, cols[h]]
            gq = (gq - qh[h] * jnp.sum(gq * qh[h], axis=-1, keepdims=True)) * (qs[h] * SCALE)
            gk = (gk - kh[h] * jnp.sum(gk * kh[h], axis=-1, keepdims=True)) * ks[h]
            gq_ref[:, cols[h]] = gq.astype(bf16)
            gk_ref[:, cols[h]] = gk.astype(bf16)
    slope = jnp.concatenate([a for a, _ in slopes], axis=1)
    last = jnp.concatenate([b for _, b in slopes], axis=1)
    gd_ref[...] = nn(triangle(True, 2), split_rows(slope, 2)) + last


def params(**more):
    return pltpu.CompilerParams(vmem_limit_bytes=VMEM_LIMIT, **more)


def relay(n, forward, maps, add):
    heads = maps.shape[0]
    whole = pl.BlockSpec(memory_space=pltpu.VMEM)
    return pl.pallas_call(
        functools.partial(relay_kernel, n, forward),
        out_shape=jax.ShapeDtypeStruct((heads, DV, DK), bf16),
        in_specs=[whole, whole],
        out_specs=whole,
        scratch_shapes=[
            pltpu.VMEM((heads, DV, DK), bf16),
            pltpu.VMEM((heads, DV, DK), bf16),
            pltpu.SemaphoreType.DMA((heads,)),
            pltpu.SemaphoreType.DMA((heads,)),
        ],
        compiler_params=params(collective_id=0 if forward else 1, has_side_effects=True),
        name="relay_forward" if forward else "relay_back",
    )(maps, add)


def per_device(
    n, queries, keys, values, decay, beta, wy_inverse, out_gate, norm_gain, out_proj, grad_out,
    resets,
):
    tokens, width = queries.shape
    heads = beta.shape[0]
    count = tokens // GROUP
    together = 4 if heads % 4 == 0 else 1
    gathered = lax.all_gather(grad_out, "head", axis=1, tiled=True)
    beta_rows = beta.T

    def rows(step):
        return (step, 0)

    def rows_back(step):
        return (count - 1 - step, 0)

    scalar = pl.BlockSpec(memory_space=pltpu.SMEM)
    tile = pl.BlockSpec((GROUP, width), rows)
    out_local, maps, enter, total = pl.pallas_call(
        functools.partial(local_kernel, heads, together),
        grid=(count,),
        in_specs=[
            scalar, tile, tile, tile, tile,
            pl.BlockSpec((GROUP, heads), rows),
            pl.BlockSpec((1, GROUP, heads * GROUP), lambda i: (i, 0, 0)),
        ],
        out_specs=[
            tile, tile,
            pl.BlockSpec((1, heads, DV + DK, DK), lambda i: (i, 0, 0, 0)),
            pl.BlockSpec((heads, DV + DK, DK), lambda i: (0, 0, 0)),
        ],
        out_shape=[
            jax.ShapeDtypeStruct((tokens, width), f32),
            jax.ShapeDtypeStruct((tokens, width), bf16),
            jax.ShapeDtypeStruct((count, heads, DV + DK, DK), bf16),
            jax.ShapeDtypeStruct((heads, DV + DK, DK), f32),
        ],
        scratch_shapes=[pltpu.VMEM((heads, DV + DK, DK), f32)],
        compiler_params=params(),
        name="local",
    )(resets, queries, keys, values, decay, beta_rows, wy_inverse)

    state_in = relay(n, True, total, total)

    upstream = lax.dot_general(
        gathered, out_proj, (((1,), (1,)), ((), ())), preferred_element_type=f32
    )
    column = pl.BlockSpec((tokens, DV), lambda h: (0, h))
    square = pl.BlockSpec((1, DV, DK), lambda h: (h, 0, 0))
    grad_raw, grad_gate, rest = pl.pallas_call(
        norm_kernel,
        grid=(heads,),
        in_specs=[
            column, column, square, column, column,
            pl.BlockSpec((1, DV), lambda h: (0, 0)),
        ],
        out_specs=[column, column, square],
        out_shape=[
            jax.ShapeDtypeStruct((tokens, width), bf16),
            jax.ShapeDtypeStruct((tokens, width), bf16),
            jax.ShapeDtypeStruct((heads, DV, DK), f32),
        ],
        compiler_params=params(),
        name="norm",
    )(out_local, maps, state_in, upstream, out_gate, norm_gain.reshape(1, DV))

    state_grad = relay(n, False, total, rest)

    tile = pl.BlockSpec((GROUP, width), rows_back)
    whole = pl.BlockSpec((heads, DV, DK), lambda i: (0, 0, 0))
    thin = pl.BlockSpec((GROUP, heads), rows_back)
    grad_query, grad_key, grad_value, grad_decay, grad_beta = pl.pallas_call(
        functools.partial(grad_kernel, heads, together),
        grid=(count,),
        in_specs=[
            scalar, tile, tile, tile, tile, thin,
            pl.BlockSpec((1, GROUP, heads * GROUP), lambda i: (count - 1 - i, 0, 0)),
            tile,
            pl.BlockSpec((1, heads, DV + DK, DK), lambda i: (count - 1 - i, 0, 0, 0)),
            whole, whole,
        ],
        out_specs=[tile, tile, tile, tile, thin],
        out_shape=[
            jax.ShapeDtypeStruct((tokens, width), bf16),
            jax.ShapeDtypeStruct((tokens, width), bf16),
            jax.ShapeDtypeStruct((tokens, width), bf16),
            jax.ShapeDtypeStruct((tokens, width), f32),
            jax.ShapeDtypeStruct((tokens, heads), f32),
        ],
        scratch_shapes=[pltpu.VMEM((heads, DV, DK), f32)],
        compiler_params=params(),
        name="grad",
    )(
        resets, queries, keys, values, decay, beta_rows, wy_inverse, grad_raw, enter, state_in,
        state_grad,
    )
    return (grad_query, grad_key, grad_value, grad_decay, grad_beta.T, grad_gate)


def solution(mesh):
    tokens_heads = P("seq", "head")
    return jax.shard_map(
        functools.partial(per_device, mesh.shape["seq"]),
        mesh=mesh,
        in_specs=(
            tokens_heads, tokens_heads, tokens_heads, tokens_heads,
            P("head", "seq"), P("seq", None, "head"), tokens_heads, P(), P("head", None),
            tokens_heads, P("seq"),
        ),
        out_specs=(
            tokens_heads, tokens_heads, tokens_heads, tokens_heads, P("head", "seq"), tokens_heads,
        ),
        check_vma=False,
    )
```

```python
import functools

import jax
import jax.numpy as jnp
from jax import lax
from jax.experimental import pallas as pl
from jax.experimental.pallas import tpu as pltpu
from jax.sharding import PartitionSpec as P

DK = 128
DV = 128
GROUP = 64
SCALE = DK ** (-0.5)
MESH = pl.DeviceIdType.MESH
VMEM_LIMIT = 48 * 1024 * 1024
f32 = jnp.float32
bf16 = jnp.bfloat16


def nn(a, b):
    return lax.dot_general(
        a.astype(bf16), b.astype(bf16), (((1,), (0,)), ((), ())), preferred_element_type=f32
    )


def nt(a, b):
    return lax.dot_general(
        a.astype(bf16), b.astype(bf16), (((1,), (1,)), ((), ())), preferred_element_type=f32
    )


def tn(a, b):
    return lax.dot_general(
        a.astype(bf16), b.astype(bf16), (((0,), (0,)), ((), ())), preferred_element_type=f32
    )


def triangle(upper, copies):
    rows = lax.broadcasted_iota(jnp.int32, (GROUP, GROUP), 0)
    cols = lax.broadcasted_iota(jnp.int32, (GROUP, GROUP), 1)
    keep = (cols >= rows) if upper else (cols <= rows)
    one = keep.astype(f32).astype(bf16)
    return jnp.concatenate([one] * copies, axis=1)


def lower_only(x):
    rows = lax.broadcasted_iota(jnp.int32, x.shape, 0)
    cols = lax.broadcasted_iota(jnp.int32, x.shape, 1)
    return jnp.where(cols <= rows, x, 0.0)


def split_rows(x, parts):
    out = []
    for _ in range(parts):
        piece = x.astype(bf16)
        out.append(piece)
        x = x - piece.astype(f32)
    return jnp.concatenate(out, axis=0)


def cumulative(decay):
    return nn(triangle(False, 3), split_rows(decay, 3))


def unit(x):
    scale = lax.rsqrt(jnp.sum(x * x, axis=-1, keepdims=True) + 1e-06)
    return x * scale, scale


def local_kernel(
    heads, together, resets, q_ref, k_ref, v_ref, g_ref, b_ref, w_ref,
    out_ref, map_ref, enter_ref, total_ref, state,
):
    step = pl.program_id(0)

    @pl.when(step == 0)
    def _():
        eye = (
            lax.broadcasted_iota(jnp.int32, (DK, DK), 0)
            == lax.broadcasted_iota(jnp.int32, (DK, DK), 1)
        ).astype(f32)
        for h in range(heads):
            state[h, :DV] = jnp.zeros((DV, DK), f32)
            state[h, DV:] = eye

    keep = jnp.where(step == resets[0], 0.0, 1.0)
    cumul = cumulative(g_ref[...])
    grow = jnp.exp(cumul)
    shrink = jnp.exp(-cumul)
    for first in range(0, heads, together):
        hs = list(range(first, first + together))
        cols = {h: slice(h * DK, (h + 1) * DK) for h in hs}
        entry, both, inv, tail, low, pred, scores, target, update = ({} for _ in range(9))
        for h in hs:
            entry[h] = state[h] * keep
            enter_ref[0, h] = entry[h].astype(bf16)
            qu = unit(q_ref[:, cols[h]].astype(f32))[0] * SCALE
            ku = unit(k_ref[:, cols[h]].astype(f32))[0]
            up = grow[:, cols[h]]
            both[h] = jnp.concatenate([(ku * up).astype(bf16), (qu * up).astype(bf16)], axis=0)
            ki = ku * shrink[:, cols[h]]
            inv[h] = ki.astype(bf16)
            tail[h] = (ki * up[GROUP - 1 :]).astype(bf16)
        for h in hs:
            pred[h] = nt(both[h], entry[h])
            scores[h] = lower_only(nt(both[h][GROUP:], inv[h]))
        for h in hs:
            beta = b_ref[:, h : h + 1]
            value = v_ref[:, cols[h]].astype(f32)
            top = pred[h][:GROUP]
            target[h] = jnp.concatenate(
                [beta * (value - top[:, :DV]), -(beta * top[:, DV:])], axis=1
            )
        for h in hs:
            update[h] = nn(w_ref[0, :, h * GROUP : (h + 1) * GROUP], target[h]).astype(bf16)
        for h in hs:
            result = pred[h][GROUP:] + nn(scores[h], update[h])
            out_ref[:, cols[h]] = result[:, :DV]
            map_ref[:, cols[h]] = result[:, DV:].astype(bf16)
            up = grow[GROUP - 1 :, cols[h]]
            state[h] = entry[h] * up + tn(update[h], tail[h])

    @pl.when(step == pl.num_programs(0) - 1)
    def _():
        total_ref[...] = state[...]


def relay_kernel(n, forward, map_ref, add_ref, out_ref, arrive, depart, send_sem, recv_sem):
    me = lax.axis_index("seq")
    heads = out_ref.shape[0]
    if forward:
        has_source, has_target = me > 0, me < n - 1
        source, target = me - 1, me + 1
    else:
        has_source, has_target = me < n - 1, me > 0
        source, target = me + 1, me - 1

    barrier = pltpu.get_barrier_semaphore()

    @pl.when(has_source)
    def _():
        pl.semaphore_signal(barrier, inc=1, device_id={"seq": source}, device_id_type=MESH)

    @pl.when(has_target)
    def _():
        pl.semaphore_signal(barrier, inc=1, device_id={"seq": target}, device_id_type=MESH)

    @pl.when(jnp.logical_and(me > 0, me < n - 1))
    def _():
        pl.semaphore_wait(barrier, 2)

    if n > 1:
        @pl.when(jnp.logical_or(me == 0, me == n - 1))
        def _():
            pl.semaphore_wait(barrier, 1)

    def copy(h):
        return pltpu.make_async_remote_copy(
            src_ref=depart.at[h],
            dst_ref=arrive.at[h],
            send_sem=send_sem.at[h],
            recv_sem=recv_sem.at[h],
            device_id={"seq": target},
            device_id_type=MESH,
        )

    @pl.when(jnp.logical_not(has_source))
    def _():
        out_ref[...] = jnp.zeros_like(out_ref)

    for h in range(heads):
        @pl.when(has_source)
        def _():
            copy(h).wait_recv()
            out_ref[h] = arrive[h]

        @pl.when(has_target)
        def _():
            matrix = map_ref[h, DV:]
            high = matrix.astype(bf16)
            rest = matrix - high.astype(f32)
            now = out_ref[h]
            times = nn if forward else nt
            depart[h] = (add_ref[h, :DV] + (times(now, high) + times(now, rest))).astype(bf16)
            copy(h).start()

    @pl.when(has_target)
    def _():
        for h in range(heads):
            copy(h).wait_send()


def norm_kernel(in_ref, map_ref, s_ref, up_ref, gate_ref, gain_ref, go_ref, gg_ref, rest_ref):
    maps = map_ref[...]
    out = in_ref[...] + nt(maps, s_ref[0])
    scale = lax.rsqrt(jnp.mean(out * out, axis=-1, keepdims=True) + 1e-06)
    normal = out * scale
    sig = jax.nn.sigmoid(gate_ref[...].astype(f32))
    grad = up_ref[...].astype(f32) * gain_ref[...] * sig
    gg_ref[...] = (grad * normal * (1.0 - sig)).astype(bf16)
    inner = jnp.mean(grad * normal, axis=-1, keepdims=True)
    grad_out = (scale * (grad - normal * inner)).astype(bf16)
    go_ref[...] = grad_out
    rest_ref[0] = tn(grad_out, maps)


def prepare_kernel(
    heads, together, span, q_ref, k_ref, v_ref, g_ref, b_ref, w_ref, go_ref, enter_ref, s_ref,
    *refs,
):
    gq_ref, qd_ref, low_ref, up_ref, err_ref, dup_ref, part_ref, di_ref = refs[-8:]
    step = pl.program_id(0)

    @pl.when(jnp.logical_and(step >= span[0], step < span[1]))
    def _():
        cumul = cumulative(g_ref[...])
        grow = jnp.exp(cumul)
        shrink = jnp.exp(-cumul)
        for first in range(0, heads, together):
            hs = list(range(first, first + together))
            cols = {h: slice(h * DK, (h + 1) * DK) for h in hs}
            low, qd, kd, ki, qh, qs, err, update, scores, gout, dscore, dq, di = (
                {} for _ in range(13)
            )
            for h in hs:
                half = enter_ref[0, h]
                low[h] = (half[:DV].astype(f32) + nn(s_ref[h], half[DV:])).astype(bf16)
                low_ref[0, h] = low[h]
                qh[h], qs[h] = unit(q_ref[:, cols[h]].astype(f32))
                kh = unit(k_ref[:, cols[h]].astype(f32))[0]
                up = grow[:, cols[h]]
                qd[h] = qh[h] * SCALE * up
                kd[h] = (kh * up).astype(bf16)
                ki[h] = kh * shrink[:, cols[h]]
                qd_ref[:, cols[h]] = qd[h].astype(bf16)
                gout[h] = go_ref[:, cols[h]]
            for h in hs:
                scores[h] = lower_only(nt(qd[h], ki[h])).astype(bf16)
                err[h] = v_ref[:, cols[h]].astype(f32) - nt(kd[h], low[h])
                err_ref[:, cols[h]] = err[h].astype(bf16)
            for h in hs:
                w = w_ref[0, :, h * GROUP : (h + 1) * GROUP]
                update[h] = nn(w, b_ref[:, h : h + 1] * err[h]).astype(bf16)
                up_ref[:, cols[h]] = update[h]
                dup_ref[:, cols[h]] = tn(scores[h], gout[h]).astype(bf16)
            for h in hs:
                dscore[h] = lower_only(nt(gout[h], update[h])).astype(bf16)
            for h in hs:
                dq[h] = nn(gout[h], low[h]) + nn(dscore[h], ki[h])
                di[h] = tn(dscore[h], qd[h])
            for h in hs:
                part_ref[:, cols[h]] = dq[h] * qd[h] - di[h] * ki[h]
                di_ref[:, cols[h]] = (di[h] * shrink[:, cols[h]]).astype(bf16)
                gq = dq[h] * grow[:, cols[h]]
                gq = (gq - qh[h] * jnp.sum(gq * qh[h], axis=-1, keepdims=True)) * (qs[h] * SCALE)
                gq_ref[:, cols[h]] = gq.astype(bf16)


def grad_kernel(
    heads, together, resets, k_ref, g_ref, b_ref, w_ref, go_ref, qd_ref, low_ref, up_ref, err_ref,
    dup_ref, part_ref, di_ref, ds_ref, gk_ref, gv_ref, gd_ref, gb_ref, state,
):
    step = pl.program_id(0)
    chunk = pl.num_programs(0) - 1 - step

    @pl.when(step == 0)
    def _():
        state[...] = ds_ref[...].astype(f32)

    keep = jnp.where(chunk == resets[0], 0.0, 1.0)
    cumul = cumulative(g_ref[...])
    grow = jnp.exp(cumul)
    shrink = jnp.exp(-cumul)
    slopes = []
    for first in range(0, heads, together):
        hs = list(range(first, first + together))
        cols = {h: slice(h * DK, (h + 1) * DK) for h in hs}
        kd, kt, kh, ks, dup, dtar, dval, past, dk, dt, nxt = ({} for _ in range(11))
        for h in hs:
            kh[h], ks[h] = unit(k_ref[:, cols[h]].astype(f32))
            up = grow[:, cols[h]]
            kd[h] = kh[h] * up
            kt[h] = kh[h] * shrink[:, cols[h]] * up[GROUP - 1 :]
            nxt[h] = state[h]
        for h in hs:
            dup[h] = dup_ref[:, cols[h]].astype(f32) + nt(kt[h], nxt[h])
        for h in hs:
            dtar[h] = tn(w_ref[0, :, h * GROUP : (h + 1) * GROUP], dup[h])
            dt[h] = nn(up_ref[:, cols[h]], nxt[h])
        for h in hs:
            dval[h] = (b_ref[:, h : h + 1] * dtar[h]).astype(bf16)
            gv_ref[:, cols[h]] = dval[h]
            gb_ref[:, h : h + 1] = jnp.sum(
                dtar[h] * err_ref[:, cols[h]].astype(f32), axis=-1, keepdims=True
            )
        for h in hs:
            both = jnp.concatenate([go_ref[:, cols[h]], -dval[h]], axis=0)
            back = jnp.concatenate([qd_ref[:, cols[h]], kd[h].astype(bf16)], axis=0)
            past[h] = nxt[h] * grow[GROUP - 1 :, cols[h]]
            state[h] = (past[h] + tn(both, back)) * keep
            dk[h] = -nn(dval[h], low_ref[0, h])
        for h in hs:
            up = grow[:, cols[h]]
            tailed = dt[h] * kt[h]
            last = jnp.sum(past[h] * low_ref[0, h].astype(f32), axis=0, keepdims=True) + jnp.sum(
                tailed, axis=0, keepdims=True
            )
            slopes.append((part_ref[:, cols[h]] + dk[h] * kd[h] - tailed, last))
            gk = dk[h] * up + dt[h] * (up[GROUP - 1 :] * shrink[:, cols[h]])
            gk = gk + di_ref[:, cols[h]].astype(f32)
            gk = (gk - kh[h] * jnp.sum(gk * kh[h], axis=-1, keepdims=True)) * ks[h]
            gk_ref[:, cols[h]] = gk.astype(bf16)
    slope = jnp.concatenate([a for a, _ in slopes], axis=1)
    last = jnp.concatenate([b for _, b in slopes], axis=1)
    gd_ref[...] = nn(triangle(True, 2), split_rows(slope, 2)) + last


def params(**more):
    return pltpu.CompilerParams(vmem_limit_bytes=VMEM_LIMIT, **more)


def relay(n, forward, maps, add):
    heads = maps.shape[0]
    whole = pl.BlockSpec(memory_space=pltpu.VMEM)
    return pl.pallas_call(
        functools.partial(relay_kernel, n, forward),
        out_shape=jax.ShapeDtypeStruct((heads, DV, DK), bf16),
        in_specs=[whole, whole],
        out_specs=whole,
        scratch_shapes=[
            pltpu.VMEM((heads, DV, DK), bf16),
            pltpu.VMEM((heads, DV, DK), bf16),
            pltpu.SemaphoreType.DMA((heads,)),
            pltpu.SemaphoreType.DMA((heads,)),
        ],
        compiler_params=params(collective_id=0 if forward else 1, has_side_effects=True),
        name="relay_forward" if forward else "relay_back",
    )(maps, add)


def per_device(
    n, queries, keys, values, decay, beta, wy_inverse, out_gate, norm_gain, out_proj, grad_out,
    resets,
):
    tokens, width = queries.shape
    heads = beta.shape[0]
    count = tokens // GROUP
    together = 4 if heads % 4 == 0 else 1
    gathered = lax.all_gather(grad_out, "head", axis=1, tiled=True)
    beta_rows = beta.T

    def rows(step):
        return (step, 0)

    def rows_back(step):
        return (count - 1 - step, 0)

    scalar = pl.BlockSpec(memory_space=pltpu.SMEM)
    tile = pl.BlockSpec((GROUP, width), rows)
    out_local, maps, enter, total = pl.pallas_call(
        functools.partial(local_kernel, heads, heads),
        grid=(count,),
        in_specs=[
            scalar, tile, tile, tile, tile,
            pl.BlockSpec((GROUP, heads), rows),
            pl.BlockSpec((1, GROUP, heads * GROUP), lambda i: (i, 0, 0)),
        ],
        out_specs=[
            tile, tile,
            pl.BlockSpec((1, heads, DV + DK, DK), lambda i: (i, 0, 0, 0)),
            pl.BlockSpec((heads, DV + DK, DK), lambda i: (0, 0, 0)),
        ],
        out_shape=[
            jax.ShapeDtypeStruct((tokens, width), f32),
            jax.ShapeDtypeStruct((tokens, width), bf16),
            jax.ShapeDtypeStruct((count, heads, DV + DK, DK), bf16),
            jax.ShapeDtypeStruct((heads, DV + DK, DK), f32),
        ],
        scratch_shapes=[pltpu.VMEM((heads, DV + DK, DK), f32)],
        compiler_params=params(),
        name="local",
    )(resets, queries, keys, values, decay, beta_rows, wy_inverse)

    state_in = relay(n, True, total, total)

    upstream = lax.dot_general(
        gathered, out_proj, (((1,), (1,)), ((), ())), preferred_element_type=bf16
    )
    column = pl.BlockSpec((tokens, DV), lambda h: (0, h))
    square = pl.BlockSpec((1, DV, DK), lambda h: (h, 0, 0))
    grad_raw, grad_gate, rest = pl.pallas_call(
        norm_kernel,
        grid=(heads,),
        in_specs=[
            column, column, square, column, column,
            pl.BlockSpec((1, DV), lambda h: (0, 0)),
        ],
        out_specs=[column, column, square],
        out_shape=[
            jax.ShapeDtypeStruct((tokens, width), bf16),
            jax.ShapeDtypeStruct((tokens, width), bf16),
            jax.ShapeDtypeStruct((heads, DV, DK), f32),
        ],
        compiler_params=params(),
        name="norm",
    )(out_local, maps, state_in, upstream, out_gate, norm_gain.reshape(1, DV))

    whole = pl.BlockSpec((heads, DV, DK), lambda i, *_: (0, 0, 0))

    def prepare(start, stop, earlier):
        def chunk(i, span):
            return jnp.minimum(jnp.maximum(i, span[0]), span[1] - 1)

        def at(i, span):
            return (chunk(i, span), 0)

        block = pl.BlockSpec((GROUP, width), at)
        low = pl.BlockSpec((1, heads, DV, DK), lambda i, span: (chunk(i, span), 0, 0, 0))
        any_place = pl.BlockSpec(memory_space=pl.ANY)
        wide = jax.ShapeDtypeStruct((tokens, width), bf16)
        out_shape = [
            wide, wide, jax.ShapeDtypeStruct((count, heads, DV, DK), bf16), wide, wide, wide,
            jax.ShapeDtypeStruct((tokens, width), f32), wide,
        ]
        inputs = (
            queries, keys, values, decay, beta_rows, wy_inverse, grad_raw, enter, state_in,
        )
        return pl.pallas_call(
            functools.partial(prepare_kernel, heads, together),
            grid_spec=pltpu.PrefetchScalarGridSpec(
                num_scalar_prefetch=1,
                grid=(count,),
                in_specs=[
                    block, block, block, block,
                    pl.BlockSpec((GROUP, heads), at),
                    pl.BlockSpec((1, GROUP, heads * GROUP), lambda i, span: (chunk(i, span), 0, 0)),
                    block,
                    pl.BlockSpec(
                        (1, heads, DV + DK, DK), lambda i, span: (chunk(i, span), 0, 0, 0)
                    ),
                    whole,
                ]
                + [any_place] * len(earlier),
                out_specs=[block, block, low, block, block, block, block, block],
            ),
            out_shape=out_shape,
            input_output_aliases={1 + len(inputs) + i: i for i in range(len(earlier))},
            compiler_params=params(),
            name="prepare",
        )(jnp.stack([start, stop]), *inputs, *earlier)

    away = n - 1 - lax.axis_index("seq")
    ahead = jnp.minimum(jnp.maximum(2 * away - 1, 1), count - 1).astype(jnp.int32)
    begun = prepare(jnp.int32(0), ahead, ())
    begun, rest = lax.optimization_barrier((begun, rest))
    state_grad = relay(n, False, total, rest)
    begun, state_grad = lax.optimization_barrier((begun, state_grad))
    grad_query, qd, low, update, err, dup, part, di = prepare(
        ahead, jnp.int32(count), tuple(begun)
    )

    tile = pl.BlockSpec((GROUP, width), rows_back)
    thin = pl.BlockSpec((GROUP, heads), rows_back)
    grad_key, grad_value, grad_decay, grad_beta = pl.pallas_call(
        functools.partial(grad_kernel, heads, together),
        grid=(count,),
        in_specs=[
            scalar, tile, tile, thin,
            pl.BlockSpec((1, GROUP, heads * GROUP), lambda i: (count - 1 - i, 0, 0)),
            tile, tile,
            pl.BlockSpec((1, heads, DV, DK), lambda i: (count - 1 - i, 0, 0, 0)),
            tile, tile, tile, tile, tile, whole,
        ],
        out_specs=[tile, tile, tile, thin],
        out_shape=[
            jax.ShapeDtypeStruct((tokens, width), bf16),
            jax.ShapeDtypeStruct((tokens, width), bf16),
            jax.ShapeDtypeStruct((tokens, width), f32),
            jax.ShapeDtypeStruct((tokens, heads), f32),
        ],
        scratch_shapes=[pltpu.VMEM((heads, DV, DK), f32)],
        compiler_params=params(),
        name="grad",
    )(
        resets, keys, decay, beta_rows, wy_inverse, grad_raw, qd, low, update, err, dup, part, di,
        state_grad,
    )
    return (grad_query, grad_key, grad_value, grad_decay, grad_beta.T, grad_gate)


def solution(mesh):
    tokens_heads = P("seq", "head")
    return jax.shard_map(
        functools.partial(per_device, mesh.shape["seq"]),
        mesh=mesh,
        in_specs=(
            tokens_heads, tokens_heads, tokens_heads, tokens_heads,
            P("head", "seq"), P("seq", None, "head"), tokens_heads, P(), P("head", None),
            tokens_heads, P("seq"),
        ),
        out_specs=(
            tokens_heads, tokens_heads, tokens_heads, tokens_heads, P("head", "seq"), tokens_heads,
        ),
        check_vma=False,
    )
```

```python
import functools

import jax
import jax.numpy as jnp
from jax import lax
from jax.experimental import pallas as pl
from jax.experimental.pallas import tpu as pltpu
from jax.sharding import PartitionSpec as P

DK = 128
DV = 128
GROUP = 64
SCALE = DK ** (-0.5)
MESH = pl.DeviceIdType.MESH
VMEM_LIMIT = 63 * 1024 * 1024
ROWS = 128
f32 = jnp.float32
bf16 = jnp.bfloat16


def nn(a, b):
    return lax.dot_general(
        a.astype(bf16), b.astype(bf16), (((1,), (0,)), ((), ())), preferred_element_type=f32
    )


def nt(a, b):
    return lax.dot_general(
        a.astype(bf16), b.astype(bf16), (((1,), (1,)), ((), ())), preferred_element_type=f32
    )


def tn(a, b):
    return lax.dot_general(
        a.astype(bf16), b.astype(bf16), (((0,), (0,)), ((), ())), preferred_element_type=f32
    )


def triangle(upper, copies):
    rows = lax.broadcasted_iota(jnp.int32, (GROUP, GROUP), 0)
    cols = lax.broadcasted_iota(jnp.int32, (GROUP, GROUP), 1)
    keep = (cols >= rows) if upper else (cols <= rows)
    one = keep.astype(f32).astype(bf16)
    return jnp.concatenate([one] * copies, axis=1)


def lower_only(x):
    rows = lax.broadcasted_iota(jnp.int32, x.shape, 0)
    cols = lax.broadcasted_iota(jnp.int32, x.shape, 1)
    return jnp.where(cols <= rows, x, 0.0)


def split_rows(x, parts):
    out = []
    for _ in range(parts):
        piece = x.astype(bf16)
        out.append(piece)
        x = x - piece.astype(f32)
    return jnp.concatenate(out, axis=0)


def cumulative(decay):
    return nn(triangle(False, 3), split_rows(decay, 3))


def unit(x):
    scale = lax.rsqrt(jnp.sum(x * x, axis=-1, keepdims=True) + 1e-06)
    return x * scale, scale


def local_kernel(
    heads, together, resets, q_ref, k_ref, v_ref, g_ref, b_ref, w_ref,
    out_ref, map_ref, enter_ref, total_ref, state,
):
    step = pl.program_id(0)

    @pl.when(step == 0)
    def _():
        eye = (
            lax.broadcasted_iota(jnp.int32, (DK, DK), 0)
            == lax.broadcasted_iota(jnp.int32, (DK, DK), 1)
        ).astype(f32)
        for h in range(heads):
            state[h, :DV] = jnp.zeros((DV, DK), f32)
            state[h, DV:] = eye

    keep = jnp.where(step == resets[0], 0.0, 1.0)
    cumul = cumulative(g_ref[...])
    grow = jnp.exp(cumul)
    shrink = jnp.exp(-cumul)
    for first in range(0, heads, together):
        hs = list(range(first, first + together))
        cols = {h: slice(h * DK, (h + 1) * DK) for h in hs}
        entry, both, inv, tail, low, pred, scores, target, update = ({} for _ in range(9))
        for h in hs:
            entry[h] = state[h] * keep
            enter_ref[0, h] = entry[h].astype(bf16)
            qu = unit(q_ref[:, cols[h]].astype(f32))[0] * SCALE
            ku = unit(k_ref[:, cols[h]].astype(f32))[0]
            up = grow[:, cols[h]]
            both[h] = jnp.concatenate([(ku * up).astype(bf16), (qu * up).astype(bf16)], axis=0)
            ki = ku * shrink[:, cols[h]]
            inv[h] = ki.astype(bf16)
            tail[h] = (ki * up[GROUP - 1 :]).astype(bf16)
        for h in hs:
            pred[h] = nt(both[h], entry[h])
            scores[h] = lower_only(nt(both[h][GROUP:], inv[h]))
        for h in hs:
            beta = b_ref[:, h : h + 1]
            value = v_ref[:, cols[h]].astype(f32)
            top = pred[h][:GROUP]
            target[h] = jnp.concatenate(
                [beta * (value - top[:, :DV]), -(beta * top[:, DV:])], axis=1
            )
        for h in hs:
            update[h] = nn(w_ref[0, :, h * GROUP : (h + 1) * GROUP], target[h]).astype(bf16)
        for h in hs:
            result = pred[h][GROUP:] + nn(scores[h], update[h])
            out_ref[:, cols[h]] = result[:, :DV]
            map_ref[:, cols[h]] = result[:, DV:].astype(bf16)
            up = grow[GROUP - 1 :, cols[h]]
            state[h] = entry[h] * up + tn(update[h], tail[h])

    @pl.when(step == pl.num_programs(0) - 1)
    def _():
        total_ref[...] = state[...]


def relay_kernel(
    n, forward, map_ref, add_ref, out_ref, arrive, depart, parts, send_sem, recv_sem
):
    me = lax.axis_index("seq")
    heads = out_ref.shape[0]
    if forward:
        has_source, has_target = me > 0, me < n - 1
        source, target = me - 1, me + 1
    else:
        has_source, has_target = me < n - 1, me > 0
        source, target = me + 1, me - 1

    barrier = pltpu.get_barrier_semaphore()

    @pl.when(has_source)
    def _():
        pl.semaphore_signal(barrier, inc=1, device_id={"seq": source}, device_id_type=MESH)

    @pl.when(has_target)
    def _():
        pl.semaphore_signal(barrier, inc=1, device_id={"seq": target}, device_id_type=MESH)

    for h in range(heads):
        matrix = map_ref[h, DV:]
        high = matrix.astype(bf16)
        rest = (matrix - high.astype(f32)).astype(bf16)
        parts[h] = jnp.concatenate([high, rest], axis=0 if forward else 1)

    @pl.when(jnp.logical_and(me > 0, me < n - 1))
    def _():
        pl.semaphore_wait(barrier, 2)

    if n > 1:
        @pl.when(jnp.logical_or(me == 0, me == n - 1))
        def _():
            pl.semaphore_wait(barrier, 1)

    def copy(h):
        return pltpu.make_async_remote_copy(
            src_ref=depart.at[h],
            dst_ref=arrive.at[h],
            send_sem=send_sem.at[h],
            recv_sem=recv_sem.at[h],
            device_id={"seq": target},
            device_id_type=MESH,
        )

    @pl.when(jnp.logical_not(has_source))
    def _():
        arrive[...] = jnp.zeros_like(arrive)

    for h in range(heads):
        @pl.when(has_source)
        def _():
            copy(h).wait_recv()

        @pl.when(has_target)
        def _():
            now = arrive[h]
            twice = jnp.concatenate([now, now], axis=1)
            moved = nn(twice, parts[h]) if forward else nt(twice, parts[h])
            depart[h] = (add_ref[h, :DV] + moved).astype(bf16)
            copy(h).start()

    out_ref[...] = arrive[...]

    @pl.when(has_target)
    def _():
        for h in range(heads):
            copy(h).wait_send()


def norm_kernel(in_ref, map_ref, s_ref, up_ref, gate_ref, gain_ref, go_ref, gg_ref, rest_ref):
    for first in range(0, in_ref.shape[0], ROWS):
        at = slice(first, first + ROWS)
        out = in_ref[at] + nt(map_ref[at], s_ref[0])
        scale = lax.rsqrt(jnp.mean(out * out, axis=-1, keepdims=True) + 1e-06)
        normal = out * scale
        sig = jax.nn.sigmoid(gate_ref[at].astype(f32))
        grad = up_ref[at].astype(f32) * gain_ref[...] * sig
        product = grad * normal
        gg_ref[at] = (product * (1.0 - sig)).astype(bf16)
        inner = jnp.mean(product, axis=-1, keepdims=True)
        go_ref[at] = (scale * (grad - normal * inner)).astype(bf16)
    rest_ref[0] = tn(go_ref[...], map_ref[...])


def grad_kernel(
    heads, together, resets, q_ref, k_ref, v_ref, g_ref, b_ref, w_ref, go_ref, enter_ref, s_ref,
    ds_ref, gq_ref, gk_ref, gv_ref, gd_ref, gb_ref, state,
):
    step = pl.program_id(0)
    chunk = pl.num_programs(0) - 1 - step

    @pl.when(step == 0)
    def _():
        state[...] = ds_ref[...].astype(f32)

    keep = jnp.where(chunk == resets[0], 0.0, 1.0)
    cumul = cumulative(g_ref[...])
    grow = jnp.exp(cumul)
    shrink = jnp.exp(-cumul)
    slopes = []
    for first in range(0, heads, together):
        hs = list(range(first, first + together))
        cols = {h: slice(h * DK, (h + 1) * DK) for h in hs}
        (entry, qd, kd, ki, kt, qh, kh, qs, ks, lows, err, update, scores, dscore, dup, dtar, dval,
         gout, past, dq, dk, di, dt, nxt, w) = ({} for _ in range(25))
        for h in hs:
            half = enter_ref[0, h]
            entry[h] = half[:DV].astype(f32) + nn(s_ref[h], half[DV:])
            qh[h], qs[h] = unit(q_ref[:, cols[h]].astype(f32))
            kh[h], ks[h] = unit(k_ref[:, cols[h]].astype(f32))
            up = grow[:, cols[h]]
            qd[h] = qh[h] * SCALE * up
            kd[h] = kh[h] * up
            ki[h] = kh[h] * shrink[:, cols[h]]
            kt[h] = ki[h] * up[GROUP - 1 :]
            gout[h] = go_ref[:, cols[h]]
            w[h] = w_ref[0, :, h * GROUP : (h + 1) * GROUP].astype(bf16)
            nxt[h] = state[h]
        for h in hs:
            lows[h] = entry[h].astype(bf16)
            scores[h] = lower_only(nt(qd[h], ki[h])).astype(bf16)
            err[h] = v_ref[:, cols[h]].astype(f32) - nt(kd[h], lows[h])
        for h in hs:
            update[h] = nn(w[h], b_ref[:, h : h + 1] * err[h]).astype(bf16)
            dup[h] = tn(scores[h], gout[h]) + nt(kt[h], nxt[h])
        for h in hs:
            dtar[h] = tn(w[h], dup[h])
            dscore[h] = lower_only(nt(gout[h], update[h])).astype(bf16)
        for h in hs:
            dval[h] = b_ref[:, h : h + 1] * dtar[h]
            gv_ref[:, cols[h]] = dval[h].astype(bf16)
            gb_ref[:, h : h + 1] = jnp.sum(dtar[h] * err[h], axis=-1, keepdims=True)
        for h in hs:
            both = jnp.concatenate([gout[h], -dval[h].astype(bf16)], axis=0)
            back = jnp.concatenate([qd[h].astype(bf16), kd[h].astype(bf16)], axis=0)
            up = grow[GROUP - 1 :, cols[h]]
            past[h] = nxt[h] * up
            state[h] = (past[h] + tn(both, back)) * keep
            through = nn(both, lows[h])
            dq[h] = through[:GROUP] + nn(dscore[h], ki[h])
            dk[h] = through[GROUP:]
            di[h] = tn(dscore[h], qd[h])
            dt[h] = nn(update[h], nxt[h])
        for h in hs:
            up = grow[:, cols[h]]
            tailed = dt[h] * kt[h]
            last = jnp.sum(past[h] * entry[h], axis=0, keepdims=True) + jnp.sum(
                tailed, axis=0, keepdims=True
            )
            slope = dq[h] * qd[h] + dk[h] * kd[h] - di[h] * ki[h] - tailed
            slopes.append((slope, last))
            gq = dq[h] * up
            gk = dk[h] * up + (di[h] + dt[h] * up[GROUP - 1 :]) * shrink[:, cols[h]]
            gq = (gq - qh[h] * jnp.sum(gq * qh[h], axis=-1, keepdims=True)) * (qs[h] * SCALE)
            gk = (gk - kh[h] * jnp.sum(gk * kh[h], axis=-1, keepdims=True)) * ks[h]
            gq_ref[:, cols[h]] = gq.astype(bf16)
            gk_ref[:, cols[h]] = gk.astype(bf16)
    slope = jnp.concatenate([a for a, _ in slopes], axis=1)
    last = jnp.concatenate([b for _, b in slopes], axis=1)
    gd_ref[...] = nn(triangle(True, 2), split_rows(slope, 2)) + last


def params(**more):
    return pltpu.CompilerParams(vmem_limit_bytes=VMEM_LIMIT, **more)


def relay(n, forward, maps, add):
    heads = maps.shape[0]
    whole = pl.BlockSpec(memory_space=pltpu.VMEM)
    return pl.pallas_call(
        functools.partial(relay_kernel, n, forward),
        out_shape=jax.ShapeDtypeStruct((heads, DV, DK), bf16),
        in_specs=[whole, whole],
        out_specs=whole,
        scratch_shapes=[
            pltpu.VMEM((heads, DV, DK), bf16),
            pltpu.VMEM((heads, DV, DK), bf16),
            pltpu.VMEM((heads, 2 * DK, DK) if forward else (heads, DK, 2 * DK), bf16),
            pltpu.SemaphoreType.DMA((heads,)),
            pltpu.SemaphoreType.DMA((heads,)),
        ],
        compiler_params=params(collective_id=0 if forward else 1, has_side_effects=True),
        name="relay_forward" if forward else "relay_back",
    )(maps, add)


def per_device(
    n, queries, keys, values, decay, beta, wy_inverse, out_gate, norm_gain, out_proj, grad_out,
    resets,
):
    tokens, width = queries.shape
    heads = beta.shape[0]
    count = tokens // GROUP
    together = heads
    gathered = lax.all_gather(grad_out, "head", axis=1, tiled=True)
    beta_rows = beta.T

    def rows(step):
        return (step, 0)

    def rows_back(step):
        return (count - 1 - step, 0)

    scalar = pl.BlockSpec(memory_space=pltpu.SMEM)
    tile = pl.BlockSpec((GROUP, width), rows)
    out_local, maps, enter, total = pl.pallas_call(
        functools.partial(local_kernel, heads, together),
        grid=(count,),
        in_specs=[
            scalar, tile, tile, tile, tile,
            pl.BlockSpec((GROUP, heads), rows),
            pl.BlockSpec((1, GROUP, heads * GROUP), lambda i: (i, 0, 0)),
        ],
        out_specs=[
            tile, tile,
            pl.BlockSpec((1, heads, DV + DK, DK), lambda i: (i, 0, 0, 0)),
            pl.BlockSpec((heads, DV + DK, DK), lambda i: (0, 0, 0)),
        ],
        out_shape=[
            jax.ShapeDtypeStruct((tokens, width), f32),
            jax.ShapeDtypeStruct((tokens, width), bf16),
            jax.ShapeDtypeStruct((count, heads, DV + DK, DK), bf16),
            jax.ShapeDtypeStruct((heads, DV + DK, DK), f32),
        ],
        scratch_shapes=[pltpu.VMEM((heads, DV + DK, DK), f32)],
        compiler_params=params(),
        name="local",
    )(resets, queries, keys, values, decay, beta_rows, wy_inverse)

    state_in = relay(n, True, total, total)

    upstream = lax.dot_general(
        gathered, out_proj, (((1,), (1,)), ((), ())), preferred_element_type=bf16
    )
    column = pl.BlockSpec((tokens, DV), lambda h: (0, h))
    square = pl.BlockSpec((1, DV, DK), lambda h: (h, 0, 0))
    grad_raw, grad_gate, rest = pl.pallas_call(
        norm_kernel,
        grid=(heads,),
        in_specs=[
            column, column, square, column, column,
            pl.BlockSpec((1, DV), lambda h: (0, 0)),
        ],
        out_specs=[column, column, square],
        out_shape=[
            jax.ShapeDtypeStruct((tokens, width), bf16),
            jax.ShapeDtypeStruct((tokens, width), bf16),
            jax.ShapeDtypeStruct((heads, DV, DK), f32),
        ],
        compiler_params=params(),
        name="norm",
    )(out_local, maps, state_in, upstream, out_gate, norm_gain.reshape(1, DV))

    state_grad = relay(n, False, total, rest)

    tile = pl.BlockSpec((GROUP, width), rows_back)
    whole = pl.BlockSpec((heads, DV, DK), lambda i: (0, 0, 0))
    thin = pl.BlockSpec((GROUP, heads), rows_back)
    grad_query, grad_key, grad_value, grad_decay, grad_beta = pl.pallas_call(
        functools.partial(grad_kernel, heads, together),
        grid=(count,),
        in_specs=[
            scalar, tile, tile, tile, tile, thin,
            pl.BlockSpec((1, GROUP, heads * GROUP), lambda i: (count - 1 - i, 0, 0)),
            tile,
            pl.BlockSpec((1, heads, DV + DK, DK), lambda i: (count - 1 - i, 0, 0, 0)),
            whole, whole,
        ],
        out_specs=[tile, tile, tile, tile, thin],
        out_shape=[
            jax.ShapeDtypeStruct((tokens, width), bf16),
            jax.ShapeDtypeStruct((tokens, width), bf16),
            jax.ShapeDtypeStruct((tokens, width), bf16),
            jax.ShapeDtypeStruct((tokens, width), f32),
            jax.ShapeDtypeStruct((tokens, heads), f32),
        ],
        scratch_shapes=[pltpu.VMEM((heads, DV, DK), f32)],
        compiler_params=params(),
        name="grad",
    )(
        resets, queries, keys, values, decay, beta_rows, wy_inverse, grad_raw, enter, state_in,
        state_grad,
    )
    return (grad_query, grad_key, grad_value, grad_decay, grad_beta.T, grad_gate)


def solution(mesh):
    tokens_heads = P("seq", "head")
    return jax.shard_map(
        functools.partial(per_device, mesh.shape["seq"]),
        mesh=mesh,
        in_specs=(
            tokens_heads, tokens_heads, tokens_heads, tokens_heads,
            P("head", "seq"), P("seq", None, "head"), tokens_heads, P(), P("head", None),
            tokens_heads, P("seq"),
        ),
        out_specs=(
            tokens_heads, tokens_heads, tokens_heads, tokens_heads, P("head", "seq"), tokens_heads,
        ),
        check_vma=False,
    )
```

```python
import functools

import jax
import jax.numpy as jnp
from jax import lax
from jax.experimental import pallas as pl
from jax.experimental.pallas import tpu as pltpu
from jax.sharding import PartitionSpec as P

DK = 128
DV = 128
GROUP = 64
SCALE = DK ** (-0.5)
MESH = pl.DeviceIdType.MESH
VMEM_LIMIT = 63 * 1024 * 1024
ROWS = 128
f32 = jnp.float32
bf16 = jnp.bfloat16


def nn(a, b):
    return lax.dot_general(
        a.astype(bf16), b.astype(bf16), (((1,), (0,)), ((), ())), preferred_element_type=f32
    )


def nt(a, b):
    return lax.dot_general(
        a.astype(bf16), b.astype(bf16), (((1,), (1,)), ((), ())), preferred_element_type=f32
    )


def tn(a, b):
    return lax.dot_general(
        a.astype(bf16), b.astype(bf16), (((0,), (0,)), ((), ())), preferred_element_type=f32
    )


def triangle(upper, copies):
    rows = lax.broadcasted_iota(jnp.int32, (GROUP, GROUP), 0)
    cols = lax.broadcasted_iota(jnp.int32, (GROUP, GROUP), 1)
    keep = (cols >= rows) if upper else (cols <= rows)
    one = keep.astype(f32).astype(bf16)
    return jnp.concatenate([one] * copies, axis=1)


def lower_only(x):
    rows = lax.broadcasted_iota(jnp.int32, x.shape, 0)
    cols = lax.broadcasted_iota(jnp.int32, x.shape, 1)
    return jnp.where(cols <= rows, x, 0.0)


def split_rows(x, parts):
    out = []
    for _ in range(parts):
        piece = x.astype(bf16)
        out.append(piece)
        x = x - piece.astype(f32)
    return jnp.concatenate(out, axis=0)


def cumulative(decay):
    return nn(triangle(False, 3), split_rows(decay, 3))


def unit(x):
    scale = lax.rsqrt(jnp.sum(x * x, axis=-1, keepdims=True) + 1e-06)
    return x * scale, scale


def local_kernel(
    heads, together, resets, q_ref, k_ref, v_ref, g_ref, b_ref, w_ref,
    out_ref, map_ref, enter_ref, offset_ref, matrix_ref, state,
):
    step = pl.program_id(0)

    @pl.when(step == 0)
    def _():
        eye = (
            lax.broadcasted_iota(jnp.int32, (DK, DK), 0)
            == lax.broadcasted_iota(jnp.int32, (DK, DK), 1)
        ).astype(f32)
        for h in range(heads):
            state[h, :DV] = jnp.zeros((DV, DK), f32)
            state[h, DV:] = eye

    keep = jnp.where(step == resets[0], 0.0, 1.0)
    cumul = cumulative(g_ref[...])
    grow = jnp.exp(cumul)
    shrink = jnp.exp(-cumul)
    for first in range(0, heads, together):
        hs = list(range(first, first + together))
        cols = {h: slice(h * DK, (h + 1) * DK) for h in hs}
        entry, both, inv, tail, low, pred, scores, target, update = ({} for _ in range(9))
        for h in hs:
            entry[h] = state[h] * keep
            enter_ref[0, h] = entry[h].astype(bf16)
            qu = unit(q_ref[:, cols[h]].astype(f32))[0] * SCALE
            ku = unit(k_ref[:, cols[h]].astype(f32))[0]
            up = grow[:, cols[h]]
            both[h] = jnp.concatenate([(ku * up).astype(bf16), (qu * up).astype(bf16)], axis=0)
            ki = ku * shrink[:, cols[h]]
            inv[h] = ki.astype(bf16)
            tail[h] = (ki * up[GROUP - 1 :]).astype(bf16)
        for h in hs:
            pred[h] = nt(both[h], entry[h])
            scores[h] = lower_only(nt(both[h][GROUP:], inv[h]))
        for h in hs:
            beta = b_ref[:, h : h + 1]
            value = v_ref[:, cols[h]].astype(f32)
            top = pred[h][:GROUP]
            target[h] = jnp.concatenate(
                [beta * (value - top[:, :DV]), -(beta * top[:, DV:])], axis=1
            )
        for h in hs:
            update[h] = nn(w_ref[0, :, h * GROUP : (h + 1) * GROUP], target[h]).astype(bf16)
        for h in hs:
            result = pred[h][GROUP:] + nn(scores[h], update[h])
            out_ref[:, cols[h]] = result[:, :DV]
            map_ref[:, cols[h]] = result[:, DV:].astype(bf16)
            up = grow[GROUP - 1 :, cols[h]]
            state[h] = entry[h] * up + tn(update[h], tail[h])

    @pl.when(step == pl.num_programs(0) - 1)
    def _():
        for h in range(heads):
            offset_ref[h] = state[h, :DV]
            matrix_ref[h] = state[h, DV:]


def relay_kernel(
    n, forward, map_ref, add_ref, out_ref, arrive, depart, parts, send_sem, recv_sem
):
    me = lax.axis_index("seq")
    heads = out_ref.shape[0]
    if forward:
        has_source, has_target = me > 0, me < n - 1
        source, target = me - 1, me + 1
    else:
        has_source, has_target = me < n - 1, me > 0
        source, target = me + 1, me - 1

    barrier = pltpu.get_barrier_semaphore()

    @pl.when(has_source)
    def _():
        pl.semaphore_signal(barrier, inc=1, device_id={"seq": source}, device_id_type=MESH)

    @pl.when(has_target)
    def _():
        pl.semaphore_signal(barrier, inc=1, device_id={"seq": target}, device_id_type=MESH)

    for h in range(heads):
        matrix = map_ref[h]
        high = matrix.astype(bf16)
        rest = (matrix - high.astype(f32)).astype(bf16)
        parts[h] = jnp.concatenate([high, rest], axis=0 if forward else 1)

    @pl.when(jnp.logical_and(me > 0, me < n - 1))
    def _():
        pl.semaphore_wait(barrier, 2)

    if n > 1:
        @pl.when(jnp.logical_or(me == 0, me == n - 1))
        def _():
            pl.semaphore_wait(barrier, 1)

    def copy(h):
        return pltpu.make_async_remote_copy(
            src_ref=depart.at[h],
            dst_ref=arrive.at[h],
            send_sem=send_sem.at[h],
            recv_sem=recv_sem.at[h],
            device_id={"seq": target},
            device_id_type=MESH,
        )

    @pl.when(jnp.logical_not(has_source))
    def _():
        arrive[...] = jnp.zeros_like(arrive)

    for h in range(heads):
        @pl.when(has_source)
        def _():
            copy(h).wait_recv()

        @pl.when(has_target)
        def _():
            now = arrive[h]
            twice = jnp.concatenate([now, now], axis=1)
            moved = nn(twice, parts[h]) if forward else nt(twice, parts[h])
            depart[h] = (add_ref[h] + moved).astype(bf16)
            copy(h).start()

    out_ref[...] = arrive[...]

    @pl.when(has_target)
    def _():
        for h in range(heads):
            copy(h).wait_send()


def norm_kernel(in_ref, map_ref, s_ref, up_ref, gate_ref, gain_ref, go_ref, gg_ref, rest_ref):
    for first in range(0, in_ref.shape[0], ROWS):
        at = slice(first, first + ROWS)
        out = in_ref[at] + nt(map_ref[at], s_ref[0])
        scale = lax.rsqrt(jnp.mean(out * out, axis=-1, keepdims=True) + 1e-06)
        normal = out * scale
        sig = jax.nn.sigmoid(gate_ref[at].astype(f32))
        grad = up_ref[at].astype(f32) * gain_ref[...] * sig
        product = grad * normal
        gg_ref[at] = (product * (1.0 - sig)).astype(bf16)
        inner = jnp.mean(product, axis=-1, keepdims=True)
        go_ref[at] = (scale * (grad - normal * inner)).astype(bf16)
    rest_ref[0] = tn(go_ref[...], map_ref[...])


def grad_kernel(
    heads, together, resets, q_ref, k_ref, v_ref, g_ref, b_ref, w_ref, go_ref, enter_ref, s_ref,
    ds_ref, gq_ref, gk_ref, gv_ref, gd_ref, gb_ref, state,
):
    step = pl.program_id(0)
    chunk = pl.num_programs(0) - 1 - step

    @pl.when(step == 0)
    def _():
        state[...] = ds_ref[...].astype(f32)

    keep = jnp.where(chunk == resets[0], 0.0, 1.0)
    cumul = cumulative(g_ref[...])
    grow = jnp.exp(cumul)
    shrink = jnp.exp(-cumul)
    slopes = []
    for first in range(0, heads, together):
        hs = list(range(first, first + together))
        cols = {h: slice(h * DK, (h + 1) * DK) for h in hs}
        (entry, qd, kd, ki, kt, qh, kh, qs, ks, lows, err, update, scores, dscore, dup, dtar, dval,
         gout, past, dq, dk, di, dt, nxt, w) = ({} for _ in range(25))
        for h in hs:
            half = enter_ref[0, h]
            entry[h] = half[:DV].astype(f32) + nn(s_ref[h], half[DV:])
            qh[h], qs[h] = unit(q_ref[:, cols[h]].astype(f32))
            kh[h], ks[h] = unit(k_ref[:, cols[h]].astype(f32))
            up = grow[:, cols[h]]
            qd[h] = qh[h] * SCALE * up
            kd[h] = kh[h] * up
            ki[h] = kh[h] * shrink[:, cols[h]]
            kt[h] = ki[h] * up[GROUP - 1 :]
            gout[h] = go_ref[:, cols[h]]
            w[h] = w_ref[0, :, h * GROUP : (h + 1) * GROUP].astype(bf16)
            nxt[h] = state[h]
        for h in hs:
            lows[h] = entry[h].astype(bf16)
            scores[h] = lower_only(nt(qd[h], ki[h])).astype(bf16)
            err[h] = v_ref[:, cols[h]].astype(f32) - nt(kd[h], lows[h])
        for h in hs:
            update[h] = nn(w[h], b_ref[:, h : h + 1] * err[h]).astype(bf16)
            dup[h] = tn(scores[h], gout[h]) + nt(kt[h], nxt[h])
        for h in hs:
            dtar[h] = tn(w[h], dup[h])
            dscore[h] = lower_only(nt(gout[h], update[h])).astype(bf16)
        for h in hs:
            dval[h] = b_ref[:, h : h + 1] * dtar[h]
            gv_ref[:, cols[h]] = dval[h].astype(bf16)
            gb_ref[:, h : h + 1] = jnp.sum(dtar[h] * err[h], axis=-1, keepdims=True)
        for h in hs:
            both = jnp.concatenate([gout[h], -dval[h].astype(bf16)], axis=0)
            back = jnp.concatenate([qd[h].astype(bf16), kd[h].astype(bf16)], axis=0)
            up = grow[GROUP - 1 :, cols[h]]
            past[h] = nxt[h] * up
            state[h] = (past[h] + tn(both, back)) * keep
            through = nn(both, lows[h])
            dq[h] = through[:GROUP] + nn(dscore[h], ki[h])
            dk[h] = through[GROUP:]
            di[h] = tn(dscore[h], qd[h])
            dt[h] = nn(update[h], nxt[h])
        for h in hs:
            up = grow[:, cols[h]]
            tailed = dt[h] * kt[h]
            last = jnp.sum(past[h] * entry[h], axis=0, keepdims=True) + jnp.sum(
                tailed, axis=0, keepdims=True
            )
            slope = dq[h] * qd[h] + dk[h] * kd[h] - di[h] * ki[h] - tailed
            slopes.append((slope, last))
            gq = dq[h] * up
            gk = dk[h] * up + (di[h] + dt[h] * up[GROUP - 1 :]) * shrink[:, cols[h]]
            gq = (gq - qh[h] * jnp.sum(gq * qh[h], axis=-1, keepdims=True)) * (qs[h] * SCALE)
            gk = (gk - kh[h] * jnp.sum(gk * kh[h], axis=-1, keepdims=True)) * ks[h]
            gq_ref[:, cols[h]] = gq.astype(bf16)
            gk_ref[:, cols[h]] = gk.astype(bf16)
    slope = jnp.concatenate([a for a, _ in slopes], axis=1)
    last = jnp.concatenate([b for _, b in slopes], axis=1)
    gd_ref[...] = nn(triangle(True, 2), split_rows(slope, 2)) + last


def params(**more):
    return pltpu.CompilerParams(vmem_limit_bytes=VMEM_LIMIT, **more)


def relay(n, forward, maps, add):
    heads = maps.shape[0]
    whole = pl.BlockSpec(memory_space=pltpu.VMEM)
    return pl.pallas_call(
        functools.partial(relay_kernel, n, forward),
        out_shape=jax.ShapeDtypeStruct((heads, DV, DK), bf16),
        in_specs=[whole, whole],
        out_specs=whole,
        scratch_shapes=[
            pltpu.VMEM((heads, DV, DK), bf16),
            pltpu.VMEM((heads, DV, DK), bf16),
            pltpu.VMEM((heads, 2 * DK, DK) if forward else (heads, DK, 2 * DK), bf16),
            pltpu.SemaphoreType.DMA((heads,)),
            pltpu.SemaphoreType.DMA((heads,)),
        ],
        compiler_params=params(collective_id=0 if forward else 1, has_side_effects=True),
        name="relay_forward" if forward else "relay_back",
    )(maps, add)


def per_device(
    n, queries, keys, values, decay, beta, wy_inverse, out_gate, norm_gain, out_proj, grad_out,
    resets,
):
    tokens, width = queries.shape
    heads = beta.shape[0]
    count = tokens // GROUP
    together = heads
    gathered = lax.all_gather(grad_out, "head", axis=1, tiled=True)
    beta_rows = beta.T

    def rows(step):
        return (step, 0)

    def rows_back(step):
        return (count - 1 - step, 0)

    scalar = pl.BlockSpec(memory_space=pltpu.SMEM)
    tile = pl.BlockSpec((GROUP, width), rows)
    out_local, maps, enter, offset, matrix = pl.pallas_call(
        functools.partial(local_kernel, heads, together),
        grid=(count,),
        in_specs=[
            scalar, tile, tile, tile, tile,
            pl.BlockSpec((GROUP, heads), rows),
            pl.BlockSpec((1, GROUP, heads * GROUP), lambda i: (i, 0, 0)),
        ],
        out_specs=[
            tile, tile,
            pl.BlockSpec((1, heads, DV + DK, DK), lambda i: (i, 0, 0, 0)),
            pl.BlockSpec((heads, DV, DK), lambda i: (0, 0, 0)),
            pl.BlockSpec((heads, DK, DK), lambda i: (0, 0, 0)),
        ],
        out_shape=[
            jax.ShapeDtypeStruct((tokens, width), f32),
            jax.ShapeDtypeStruct((tokens, width), bf16),
            jax.ShapeDtypeStruct((count, heads, DV + DK, DK), bf16),
            jax.ShapeDtypeStruct((heads, DV, DK), f32),
            jax.ShapeDtypeStruct((heads, DK, DK), f32),
        ],
        scratch_shapes=[pltpu.VMEM((heads, DV + DK, DK), f32)],
        compiler_params=params(),
        name="local",
    )(resets, queries, keys, values, decay, beta_rows, wy_inverse)

    state_in = relay(n, True, matrix, offset)

    upstream = lax.dot_general(
        gathered, out_proj, (((1,), (1,)), ((), ())), preferred_element_type=bf16
    )
    column = pl.BlockSpec((tokens, DV), lambda h: (0, h))
    square = pl.BlockSpec((1, DV, DK), lambda h: (h, 0, 0))
    grad_raw, grad_gate, rest = pl.pallas_call(
        norm_kernel,
        grid=(heads,),
        in_specs=[
            column, column, square, column, column,
            pl.BlockSpec((1, DV), lambda h: (0, 0)),
        ],
        out_specs=[column, column, square],
        out_shape=[
            jax.ShapeDtypeStruct((tokens, width), bf16),
            jax.ShapeDtypeStruct((tokens, width), bf16),
            jax.ShapeDtypeStruct((heads, DV, DK), f32),
        ],
        compiler_params=params(),
        name="norm",
    )(out_local, maps, state_in, upstream, out_gate, norm_gain.reshape(1, DV))

    state_grad = relay(n, False, matrix, rest)

    tile = pl.BlockSpec((GROUP, width), rows_back)
    whole = pl.BlockSpec((heads, DV, DK), lambda i: (0, 0, 0))
    thin = pl.BlockSpec((GROUP, heads), rows_back)
    grad_query, grad_key, grad_value, grad_decay, grad_beta = pl.pallas_call(
        functools.partial(grad_kernel, heads, together),
        grid=(count,),
        in_specs=[
            scalar, tile, tile, tile, tile, thin,
            pl.BlockSpec((1, GROUP, heads * GROUP), lambda i: (count - 1 - i, 0, 0)),
            tile,
            pl.BlockSpec((1, heads, DV + DK, DK), lambda i: (count - 1 - i, 0, 0, 0)),
            whole, whole,
        ],
        out_specs=[tile, tile, tile, tile, thin],
        out_shape=[
            jax.ShapeDtypeStruct((tokens, width), bf16),
            jax.ShapeDtypeStruct((tokens, width), bf16),
            jax.ShapeDtypeStruct((tokens, width), bf16),
            jax.ShapeDtypeStruct((tokens, width), f32),
            jax.ShapeDtypeStruct((tokens, heads), f32),
        ],
        scratch_shapes=[pltpu.VMEM((heads, DV, DK), f32)],
        compiler_params=params(),
        name="grad",
    )(
        resets, queries, keys, values, decay, beta_rows, wy_inverse, grad_raw, enter, state_in,
        state_grad,
    )
    return (grad_query, grad_key, grad_value, grad_decay, grad_beta.T, grad_gate)


def solution(mesh):
    tokens_heads = P("seq", "head")
    return jax.shard_map(
        functools.partial(per_device, mesh.shape["seq"]),
        mesh=mesh,
        in_specs=(
            tokens_heads, tokens_heads, tokens_heads, tokens_heads,
            P("head", "seq"), P("seq", None, "head"), tokens_heads, P(), P("head", None),
            tokens_heads, P("seq"),
        ),
        out_specs=(
            tokens_heads, tokens_heads, tokens_heads, tokens_heads, P("head", "seq"), tokens_heads,
        ),
        check_vma=False,
    )
```
